32 devices in a mesh: groups: 2 (over y), wide: 4 (over z), narrow: 4 (over x, core).
Axes of the slice: x: 2, y: 2, z: 4, core: 2. Of those that a mesh axis runs over, the one named last changes fastest.
Arguments:
- hidden: bfloat16 [32, 8192], P('groups', 'wide'), parts along dimension 0, may hold values from -6 to 6
- w_query: bfloat16 [8192, 8192], P('wide', 'narrow'), may hold values from -0.0625 to 0.0625
- w_key: bfloat16 [8192, 1024], P('wide', 'narrow'), may hold values from -0.0625 to 0.0625
- w_value: bfloat16 [8192, 1024], P('wide', 'narrow'), may hold values from -0.0625 to 0.0625
- w_out: bfloat16 [8192, 8192], P('narrow', 'wide'), may hold values from -0.0625 to 0.0625
- key_cache: bfloat16 [32, 768, 8, 128], P(('groups', 'wide'), None, 'narrow'), parts along dimension 0, may hold values from -720 to 720
- value_cache: bfloat16 [32, 768, 8, 128], P(('groups', 'wide'), None, 'narrow'), parts along dimension 0, may hold values from -6 to 6
- cycle_offset: int32 [32], P(('groups', 'wide')), parts along dimension 0, may hold values from 0 to 767
- valid_length: int32 [32], P(('groups', 'wide')), parts along dimension 0, may hold values from 1 to 768, as said below
- slot_of: int32 [32], P('groups'), parts along dimension 0, may hold values from 0 to 15, as said below
Outputs:
- attn_out: bfloat16 [32, 8192], P('groups', 'wide'), parts along dimension 0
- new_keys: bfloat16 [32, 1024], P(('groups', 'wide'), 'narrow'), parts along dimension 0
- new_values: bfloat16 [32, 1024], P(('groups', 'wide'), 'narrow'), parts along dimension 0
The draws below stay inside these ranges and needn't reach their ends.
There are 2 independent parts, one for each index of `groups`. The reference program is written for one: setup_inputs(seed, part) draws one part's arguments, and reference() takes and returns one part's arrays. A program takes and returns all parts, laid end to end along the dimension named above; an argument that names none is the same for every part. Nothing has to cross between parts.
Inputs may be any that keep to these rules, and one draw needn't show every extreme that they name: Requests are in 4 microbatches of consecutive rows; each cache owner (a block of 4 consecutive slots) holds exactly 1 request of each microbatch m, at the slots owner * 4 + m + j for 0 <= j < 1; slot_of is a permutation. `valid_length`: at least one slot has a full cycle.
All inputs are finite; a program needn't handle non-finite values.
Results may differ from the reference program's by a relative error of at most 0.012.
Values may be sent and summed in bfloat16 or wider, within the bound.
No kernel may reach another device: no remote copies, remote signals or barrier semaphores. Data moves between devices by JAX's collectives and lax.ppermute only.
A program may use at most 64 MiB of HBM per device.

```python
import jax
import jax.numpy as jnp
from jax import lax

D = 8192
HQ = 64
KV = 8
HD = 128
L = 768
SLOT_MB = 1
MICRO = 4
REQ_DEV = 4
REQUESTS = 16


def draw_key_cache(key, part):
    base = jax.random.normal(jax.random.fold_in(key, 11), (REQUESTS, L, KV, HD), jnp.float32)
    base = jnp.clip(base, -6.0, 6.0)
    return base.astype(jnp.bfloat16)


def draw_valid_length(key, part):
    lengths = jax.random.randint(jax.random.fold_in(key, 21), (REQUESTS,), 1, L + 1)
    longest = jax.random.randint(jax.random.fold_in(key, 22), (), 0, REQUESTS)
    return jnp.where(jnp.arange(REQUESTS, dtype=jnp.int32) == longest, L, lengths).astype(jnp.int32)


def draw_slot_of(key, part):
    rows_block = REQUESTS // MICRO
    block_keys = jax.random.split(jax.random.fold_in(key, 31), MICRO)

    def shuffle(one_key):
        return jax.random.permutation(one_key, rows_block)
    perms = jax.vmap(shuffle)(block_keys)
    blocks = jnp.arange(MICRO, dtype=jnp.int32)[:, None]
    owner = perms // SLOT_MB
    within = perms % SLOT_MB
    slots = owner * REQ_DEV + blocks * SLOT_MB + within
    return slots.reshape(REQUESTS).astype(jnp.int32)


def touch_ends(result, stream_key, least, top_value):
    shape = result.shape
    spot = [jax.random.randint(jax.random.fold_in(stream_key, axis), (), 0, shape[axis]) for axis in range(len(shape))]
    result = result.at[tuple(spot)].set(least)
    longest = shape.index(max(shape))
    spot[longest] = (spot[longest] + 1) % shape[longest]
    return result.at[tuple(spot)].set(top_value)


def level_of(stream_key, extent, pieces, least, high):
    def one(position, parts):
        heights = jax.random.uniform(jax.random.fold_in(jax.random.fold_in(stream_key, 6), position), (parts,), jnp.float32, least / len(pieces), high / len(pieces))
        return jnp.repeat(jnp.exp(heights), extent[position] // parts).reshape((-1,) + (1,) * (len(extent) - position - 1))

    gain = one(*pieces[0])
    for cut in pieces[1:]:
        gain = gain * one(*cut)
    return gain


def gaussian(own_key, shape, width, bound, pieces=(), kind=jnp.bfloat16):
    factor_of = level_of(own_key, shape, pieces, -0.22, 0.18) if pieces else 1.0
    values = jax.random.normal(own_key, shape, jnp.float32) * width * factor_of
    return jnp.minimum(jnp.maximum(values, -bound), bound).astype(kind)


def setup_inputs(seed: int = 0, part: int = 0) -> dict:
    splits = jax.random.split(jax.random.key(seed), 11)
    part_splits = jax.random.split(jax.random.fold_in(splits[10], part), 11)
    return {
        "hidden": gaussian(part_splits[0], (REQUESTS, D), 1.0, 6.0, ((1, 4),)),
        "w_query": gaussian(splits[1], (D, HQ * HD), D ** -0.5, 0.0625, ((0, 4), (1, 4))),
        "w_key": gaussian(splits[2], (D, KV * HD), D ** -0.5, 0.0625, ((0, 4), (1, 4))),
        "w_value": gaussian(splits[3], (D, KV * HD), D ** -0.5, 0.0625, ((0, 4), (1, 4))),
        "w_out": gaussian(splits[4], (HQ * HD, D), (HQ * HD) ** -0.5, 0.0625, ((0, 4), (1, 4))),
        "key_cache": draw_key_cache(jax.random.fold_in(jax.random.fold_in(splits[10], part), 71), part),
        "value_cache": gaussian(part_splits[6], (REQUESTS, L, KV, HD), 1.0, 6.0, ((0, 4), (2, 4))),
        "cycle_offset": touch_ends(jax.random.randint(part_splits[7], (REQUESTS,), 0, L), jax.random.fold_in(part_splits[7], 1), 0, L - 1).astype(jnp.int32),
        "valid_length": draw_valid_length(jax.random.fold_in(jax.random.fold_in(splits[10], part), 71), part),
        "slot_of": draw_slot_of(jax.random.fold_in(jax.random.fold_in(splits[10], part), 71), part),
    }


def reference(hidden, w_query, w_key, w_value, w_out, key_cache, value_cache, cycle_offset, valid_length, slot_of):
    order = jnp.zeros((REQUESTS,), jnp.int32).at[slot_of].set(jnp.arange(REQUESTS, dtype=jnp.int32))
    slot_rows = hidden[order]
    queries = jnp.dot(slot_rows, w_query, preferred_element_type=jnp.float32).astype(jnp.bfloat16)
    new_keys = jnp.dot(slot_rows, w_key, preferred_element_type=jnp.float32).astype(jnp.bfloat16)
    new_values = jnp.dot(slot_rows, w_value, preferred_element_type=jnp.float32).astype(jnp.bfloat16)
    group = HQ // KV
    scale = 1.0 / jnp.sqrt(jnp.float32(HD))

    def one_slot(items):
        query_row, key_row, value_row, keys_old, values_old, offset, length = items
        keys_all = keys_old.at[offset].set(key_row.reshape(KV, HD))
        values_all = values_old.at[offset].set(value_row.reshape(KV, HD))
        query_heads = query_row.reshape(KV, group, HD).astype(jnp.float32)
        scores = jnp.einsum('kgd,jkd->kgj', query_heads, keys_all.astype(jnp.float32)) * scale
        distance = (offset - jnp.arange(L, dtype=jnp.int32)) % L
        usable = (distance < length)[None, None, :]
        masked = jnp.where(usable, scores, -jnp.inf)
        top = lax.optimization_barrier(jnp.max(masked, axis=2, keepdims=True))
        spread = jnp.where(usable, jnp.exp(masked - top), 0.0)
        probs = (spread / lax.optimization_barrier(jnp.sum(spread, axis=2, keepdims=True))).astype(jnp.bfloat16)
        mixed = jnp.einsum('kgj,jkd->kgd', probs.astype(jnp.float32), values_all.astype(jnp.float32))
        return mixed.astype(jnp.bfloat16).reshape(HQ * HD)
    heads = lax.map(one_slot, (queries, new_keys, new_values, key_cache, value_cache, cycle_offset, valid_length))
    projected = jnp.dot(heads, w_out, preferred_element_type=jnp.float32)
    attn_out = projected[slot_of].astype(jnp.bfloat16)
    return (attn_out, new_keys, new_values)
```

```python
import jax
import jax.numpy as jnp
from jax import lax
from jax.sharding import PartitionSpec as P

masked_low = -1e30
most_direct = 8


def is_direct(count):
    return count <= most_direct and count & (count - 1) == 0


def swap(block, axis, distance):
    count = lax.axis_size(axis)
    return lax.ppermute(block, axis, [(i, i ^ distance) for i in range(count)])


def tree_sum(terms):
    while len(terms) > 1:
        terms = [a + b for a, b in zip(terms[::2], terms[1::2])]
    return terms[0]


def attend(queries, keys_new, values_new, key_cache, value_cache, offset, length):
    slots, window, kv_local, head_dim = key_cache.shape
    group = queries.shape[1] // (kv_local * head_dim)
    scale = 1.0 / jnp.sqrt(jnp.float32(head_dim))
    query_heads = queries.reshape(slots, kv_local, group, head_dim)
    key_heads = keys_new.reshape(slots, kv_local, head_dim)
    value_heads = values_new.reshape(slots, kv_local, head_dim)
    cached = (
        jnp.einsum("skgd,sjkd->skgj", query_heads, key_cache, preferred_element_type=jnp.float32)
        * scale
    )
    fresh = (
        jnp.einsum("skgd,skd->skg", query_heads, key_heads, preferred_element_type=jnp.float32)
        * scale
    )
    distance = (offset[:, None] - jnp.arange(window, dtype=jnp.int32)[None, :]) % window
    usable = ((distance > 0) & (distance < length[:, None]))[:, None, None, :]
    masked = jnp.where(usable, cached, masked_low)
    top = jnp.maximum(jnp.max(masked, axis=3), fresh)
    spread = jnp.where(usable, jnp.exp(masked - top[..., None]), 0.0)
    own = jnp.exp(fresh - top)
    total = jnp.sum(spread, axis=3) + own
    weights = (spread / total[..., None]).astype(jnp.bfloat16)
    own_weight = (own / total).astype(jnp.bfloat16)
    mixed = jnp.einsum("skgj,sjkd->skgd", weights, value_cache, preferred_element_type=jnp.float32)
    mixed = (
        mixed
        + own_weight.astype(jnp.float32)[..., None] * value_heads.astype(jnp.float32)[:, :, None, :]
    )
    return mixed.astype(jnp.bfloat16).reshape(slots, -1)


def per_device(
    hidden,
    w_query,
    w_key,
    w_value,
    w_out,
    key_cache,
    value_cache,
    cycle_offset,
    valid_length,
    slot_of,
):
    requests = slot_of.shape[0]
    slots_dev = key_cache.shape[0]
    query_cols = w_query.shape[1]
    key_cols = w_key.shape[1]
    wide = lax.axis_size("wide")
    direct_wide = is_direct(wide)
    place = jnp.arange(requests, dtype=jnp.int32)
    if direct_wide:
        me = lax.axis_index("wide")
        slot_at = (me ^ (place // slots_dev)) * slots_dev + place % slots_dev
    else:
        slot_at = place
    picks = (slot_at[:, None] == slot_of[None, :]).astype(jnp.bfloat16)
    rows = jnp.dot(picks, hidden, preferred_element_type=jnp.float32).astype(jnp.bfloat16)
    parts = jnp.concatenate(
        [
            jnp.dot(rows, w_query, preferred_element_type=jnp.float32),
            jnp.dot(rows, w_key, preferred_element_type=jnp.float32),
            jnp.dot(rows, w_value, preferred_element_type=jnp.float32),
        ],
        axis=1,
    )
    if direct_wide:
        summed = tree_sum(
            [parts[:slots_dev]]
            + [
                swap(parts[d * slots_dev : (d + 1) * slots_dev], "wide", d)
                for d in range(1, wide)
            ]
        )
    else:
        summed = lax.psum_scatter(parts, "wide", scatter_dimension=0, tiled=True)
    fresh = summed.astype(jnp.bfloat16)
    queries = fresh[:, :query_cols]
    keys_out = fresh[:, query_cols : query_cols + key_cols]
    values_out = fresh[:, query_cols + key_cols :]
    heads = attend(
        queries, keys_out, values_out, key_cache, value_cache, cycle_offset, valid_length
    )
    if direct_wide:
        heads = jnp.concatenate([heads] + [swap(heads, "wide", d) for d in range(1, wide)], axis=0)
    else:
        heads = lax.all_gather(heads, "wide", axis=0, tiled=True)
    heads = jnp.dot(picks.T, heads, preferred_element_type=jnp.float32).astype(jnp.bfloat16)
    request_out = jnp.dot(heads, w_out, preferred_element_type=jnp.float32)
    narrow = lax.axis_size("narrow")
    if is_direct(narrow):
        sent = request_out.astype(jnp.bfloat16)
        attn_out = tree_sum(
            [sent.astype(jnp.float32)]
            + [swap(sent, "narrow", d).astype(jnp.float32) for d in range(1, narrow)]
        )
    else:
        attn_out = lax.psum(request_out, "narrow")
    return (attn_out.astype(jnp.bfloat16), keys_out, values_out)


def solution(mesh):
    placed = (
        P("groups", "wide"),
        P("wide", "narrow"),
        P("wide", "narrow"),
        P("wide", "narrow"),
        P("narrow", "wide"),
        P(("groups", "wide"), None, "narrow", None),
        P(("groups", "wide"), None, "narrow", None),
        P(("groups", "wide")),
        P(("groups", "wide")),
        P("groups"),
    )
    return jax.shard_map(
        per_device,
        mesh=mesh,
        in_specs=placed,
        out_specs=(
            P("groups", "wide"),
            P(("groups", "wide"), "narrow"),
            P(("groups", "wide"), "narrow"),
        ),
        check_vma=False,
    )
```

```python
import functools

import jax
import jax.numpy as jnp
from jax import lax
from jax.experimental import pallas as pl
from jax.experimental.pallas import tpu as pltpu
from jax.sharding import PartitionSpec as P

masked_low = -1e30
most_direct = 8
depth_block = 256
mebibyte = 2**20

in_hbm = pl.BlockSpec(memory_space=pltpu.MemorySpace.HBM)
in_vmem = pl.BlockSpec(memory_space=pltpu.MemorySpace.VMEM)


def kept_in_hbm(x):
    return pltpu.with_memory_space_constraint(x, pltpu.MemorySpace.HBM)


def kept_in_vmem(x):
    return pltpu.with_memory_space_constraint(x, pltpu.MemorySpace.VMEM)


def is_direct(count):
    return count <= most_direct and count & (count - 1) == 0


def swap(block, axis, distance):
    count = lax.axis_size(axis)
    return lax.ppermute(block, axis, [(i, i ^ distance) for i in range(count)])


def exchange(blocks, axis):
    count = lax.axis_size(axis)
    came = [swap(blocks[d], axis, d) for d in range(count - 1, 0, -1)]
    return [blocks[0]] + came[::-1]


def tree_sum(terms):
    while len(terms) > 1:
        terms = [a + b for a, b in zip(terms[::2], terms[1::2])]
    return terms[0]


def project_kernel(slots_dev, direct, pieces, kv_local, *refs):
    ins, refs = refs[:8], refs[8:]
    slot_hbm, offset_hbm, length_hbm, hidden_hbm, wk_hbm, wv_hbm, wq_hbm, me_ref = ins
    outs, refs = refs[:pieces], refs[pieces:]
    picks_ref, bias_ref, slot, offset, length, hidden, wk, wv, wq, rows, total, small, large = refs
    depth = wq.shape[0]
    blocks = large.shape[0]
    step = depth // blocks
    early = [
        pltpu.make_async_copy(source, target, small.at[i])
        for i, (source, target) in enumerate(
            (
                (slot_hbm, slot),
                (hidden_hbm, hidden),
                (wk_hbm, wk),
                (wv_hbm, wv),
                (offset_hbm, offset),
                (length_hbm, length),
            )
        )
    ]
    spans = [pl.ds(b * step, step) for b in range(blocks)]
    late = [
        pltpu.make_async_copy(wq_hbm.at[span], wq.at[span], large.at[b])
        for b, span in enumerate(spans)
    ]
    for copy in early + late:
        copy.start()

    early[0].wait()
    early[1].wait()
    requests = slot.shape[1]
    place = lax.broadcasted_iota(jnp.int32, (requests, requests), 0)
    if direct:
        me = me_ref[0]
        slot_at = (me ^ (place // slots_dev)) * slots_dev + place % slots_dev
    else:
        slot_at = place
    picks = (slot_at == slot[...]).astype(jnp.float32).astype(jnp.bfloat16)
    picks_ref[...] = picks
    rows[...] = jnp.dot(picks, hidden[...], preferred_element_type=jnp.float32).astype(jnp.bfloat16)

    query_cols, key_cols = wq.shape[1], wk.shape[1]
    early[2].wait()
    total[:, query_cols : query_cols + key_cols] = jnp.dot(
        rows[...], wk[...], preferred_element_type=jnp.float32
    )
    early[3].wait()
    total[:, query_cols + key_cols :] = jnp.dot(
        rows[...], wv[...], preferred_element_type=jnp.float32
    )

    early[4].wait()
    early[5].wait()
    slots, places = bias_ref.shape
    window = places // kv_local
    position = lax.broadcasted_iota(jnp.int32, (1, places), 1) // kv_local
    for s in range(slots):
        gap = offset[s] - position
        distance = jnp.where(gap < 0, gap + window, gap)
        usable = (distance > 0) & (distance < length[s])
        bias_ref[s : s + 1, :] = jnp.where(usable, 0.0, masked_low)

    for b, span in enumerate(spans):
        late[b].wait()
        part = jnp.dot(rows[:, span], wq[span, :], preferred_element_type=jnp.float32)
        if b == 0:
            total[:, :query_cols] = part
        else:
            total[:, :query_cols] += part
    size = requests // pieces
    for d, out in enumerate(outs):
        out[...] = total[d * size : (d + 1) * size, :]


def project(me, slot_of, offset, length, hidden, w_key, w_value, w_query, cache, direct, pieces):
    requests = slot_of.shape[0]
    slots, places = cache.shape[0], cache.shape[1] * cache.shape[2]
    depth, query_cols = w_query.shape
    cols = query_cols + w_key.shape[1] + w_value.shape[1]
    blocks = max(1, depth // depth_block)
    found = pl.pallas_call(
        functools.partial(project_kernel, slots, direct, pieces, cache.shape[2]),
        out_shape=[
            pltpu.VMEM((requests // pieces, cols), jnp.float32) for _ in range(pieces)
        ]
        + [pltpu.VMEM((requests, requests), jnp.bfloat16), pltpu.VMEM((slots, places), jnp.float32)],
        in_specs=[in_hbm] * 7 + [pl.BlockSpec(memory_space=pltpu.MemorySpace.SMEM)],
        out_specs=[in_vmem] * (pieces + 2),
        scratch_shapes=[
            pltpu.VMEM((1, requests), jnp.int32),
            pltpu.SMEM(offset.shape, jnp.int32),
            pltpu.SMEM(length.shape, jnp.int32),
            pltpu.VMEM(hidden.shape, jnp.bfloat16),
            pltpu.VMEM(w_key.shape, jnp.bfloat16),
            pltpu.VMEM(w_value.shape, jnp.bfloat16),
            pltpu.VMEM(w_query.shape, jnp.bfloat16),
            pltpu.VMEM(hidden.shape, jnp.bfloat16),
            pltpu.VMEM((requests, cols), jnp.float32),
            pltpu.SemaphoreType.DMA((6,)),
            pltpu.SemaphoreType.DMA((blocks,)),
        ],
        compiler_params=pltpu.CompilerParams(vmem_limit_bytes=24 * mebibyte),
        cost_estimate=pl.CostEstimate(
            flops=2 * requests * depth * cols, bytes_accessed=2 * depth * cols, transcendentals=0
        ),
    )(
        *[
            kept_in_hbm(x)
            for x in (slot_of.reshape(1, -1), offset, length, hidden, w_key, w_value, w_query)
        ],
        me.reshape(1),
    )
    return found[:pieces], found[pieces], found[pieces + 1]


def fetch_kernel(spans, count, *refs):
    sources, targets, sems = refs[:count], refs[-1 - len(spans) : -1], refs[-1]
    copies = []
    for (which, first, size, cuts), target in zip(spans, targets):
        for c in range(cuts):
            part = size // cuts
            copies.append(
                pltpu.make_async_copy(
                    sources[which].at[pl.ds(first + c * part, part)],
                    target.at[pl.ds(c * part, part)],
                    sems.at[len(copies)],
                )
            )
    for copy in copies:
        copy.start()
    for copy in copies:
        copy.wait()


def fetch(sources, spans, after):
    size = sum(2 * n * sources[w][0].size for w, _, n, _ in spans)
    return pl.pallas_call(
        functools.partial(fetch_kernel, spans, len(sources)),
        out_shape=[pltpu.VMEM((n,) + sources[w].shape[1:], sources[w].dtype) for w, _, n, _ in spans],
        in_specs=[in_hbm] * len(sources) + [in_vmem],
        out_specs=[in_vmem] * len(spans),
        scratch_shapes=[pltpu.SemaphoreType.DMA((sum(c for *_, c in spans),))],
        compiler_params=pltpu.CompilerParams(vmem_limit_bytes=24 * mebibyte),
        cost_estimate=pl.CostEstimate(flops=0, bytes_accessed=size, transcendentals=0),
    )(*[kept_in_hbm(x) for x in sources], kept_in_vmem(after))


def attend_kernel(group, parts_count, kv_local, *refs):
    parts, refs = refs[:parts_count], refs[parts_count:]
    keys, values, bias, heads_ref, keys_ref, values_ref, query_rows, mixed_rows = refs
    slots, places, head_dim = keys.shape
    rows = kv_local * group
    query_cols, key_cols = rows * head_dim, kv_local * head_dim
    fresh = tree_sum([part[...] for part in parts]).astype(jnp.bfloat16)
    keys_ref[...] = fresh[:, query_cols : query_cols + key_cols]
    values_ref[...] = fresh[:, query_cols + key_cols :]
    fresh = fresh.astype(jnp.float32)
    for h in range(rows):
        query_rows[pl.ds(h, slots, stride=rows), :] = fresh[:, h * head_dim : (h + 1) * head_dim]
    scale = 1.0 / jnp.sqrt(jnp.float32(head_dim))
    row_kv = lax.broadcasted_iota(jnp.int32, (rows, 1), 0) // group
    col_kv = lax.broadcasted_iota(jnp.int32, (1, places), 1) % kv_local
    own_head = row_kv == col_kv

    def spread_new(s, first):
        out = fresh[s : s + 1, first : first + head_dim]
        for k in range(1, kv_local):
            left = first + k * head_dim
            out = jnp.where(row_kv == k, fresh[s : s + 1, left : left + head_dim], out)
        return out

    for s in range(slots):
        query = query_rows[s * rows : (s + 1) * rows, :]
        scores = lax.dot_general(
            query.astype(jnp.bfloat16),
            keys[s],
            (((1,), (1,)), ((), ())),
            preferred_element_type=jnp.float32,
        )
        usable = own_head & (bias[s : s + 1, :] == 0.0)
        masked = jnp.where(usable, scores * scale, masked_low)
        latest = jnp.sum(query * spread_new(s, query_cols), axis=1, keepdims=True) * scale
        top = jnp.maximum(jnp.max(masked, axis=1, keepdims=True), latest)
        spread = jnp.exp(masked - top)
        own = jnp.exp(latest - top)
        total = jnp.sum(spread, axis=1, keepdims=True) + own
        weights = (spread / total).astype(jnp.bfloat16)
        own_weight = (own / total).astype(jnp.bfloat16).astype(jnp.float32)
        mixed = jnp.dot(weights, values[s], preferred_element_type=jnp.float32)
        mixed_rows[s * rows : (s + 1) * rows, :] = mixed + own_weight * spread_new(
            s, query_cols + key_cols
        )
    for h in range(rows):
        heads_ref[:, h * head_dim : (h + 1) * head_dim] = mixed_rows[
            pl.ds(h, slots, stride=rows), :
        ].astype(jnp.bfloat16)


def attend(parts, keys, values, bias, kv_local, query_cols):
    slots, places, head_dim = keys.shape
    rows = query_cols // head_dim
    key_cols = kv_local * head_dim
    return pl.pallas_call(
        functools.partial(attend_kernel, rows // kv_local, len(parts), kv_local),
        out_shape=[
            pltpu.VMEM((slots, query_cols), jnp.bfloat16),
            jax.ShapeDtypeStruct((slots, key_cols), jnp.bfloat16),
            jax.ShapeDtypeStruct((slots, key_cols), jnp.bfloat16),
        ],
        in_specs=[in_vmem] * (len(parts) + 3),
        out_specs=[in_vmem] * 3,
        scratch_shapes=[
            pltpu.VMEM((slots * rows, head_dim), jnp.float32),
            pltpu.VMEM((slots * rows, head_dim), jnp.float32),
        ],
        compiler_params=pltpu.CompilerParams(vmem_limit_bytes=24 * mebibyte),
        cost_estimate=pl.CostEstimate(
            flops=4 * slots * rows * places * head_dim,
            bytes_accessed=4 * slots * places * head_dim,
            transcendentals=slots * rows * places,
        ),
    )(*[kept_in_vmem(x) for x in (*parts, keys, values, bias)])


def output_kernel(heads_count, picks_ref, *refs):
    heads, weights, out_ref = refs[:heads_count], refs[heads_count:-1], refs[-1]
    stacked = jnp.concatenate([h[...].astype(jnp.float32) for h in heads], axis=0)
    rows = lax.dot_general(
        picks_ref[...],
        stacked.astype(jnp.bfloat16),
        (((0,), (0,)), ((), ())),
        preferred_element_type=jnp.float32,
    ).astype(jnp.bfloat16)
    found, first = None, 0
    for weight in weights:
        last = first + weight.shape[0]
        part = jnp.dot(rows[:, first:last], weight[...], preferred_element_type=jnp.float32)
        found = part if found is None else found + part
        first = last
    out_ref[...] = found.astype(out_ref.dtype)


def project_out(picks, heads, weights, dtype):
    requests = picks.shape[0]
    cols = weights[0].shape[1]
    size = sum(w.size for w in weights)
    return pl.pallas_call(
        functools.partial(output_kernel, len(heads)),
        out_shape=pltpu.VMEM((requests, cols), dtype),
        in_specs=[in_vmem] * (1 + len(heads) + len(weights)),
        out_specs=in_vmem,
        compiler_params=pltpu.CompilerParams(vmem_limit_bytes=24 * mebibyte),
        cost_estimate=pl.CostEstimate(
            flops=2 * requests * size, bytes_accessed=2 * size, transcendentals=0
        ),
    )(*[kept_in_vmem(x) for x in (picks, *heads, *weights)])


def per_device(
    hidden,
    w_query,
    w_key,
    w_value,
    w_out,
    key_cache,
    value_cache,
    cycle_offset,
    valid_length,
    slot_of,
):
    slots, window, kv_local, head_dim = key_cache.shape
    wide = lax.axis_size("wide")
    direct_wide = is_direct(wide)
    me = lax.axis_index("wide").astype(jnp.int32)
    parts, picks, bias = project(
        me,
        slot_of,
        cycle_offset,
        valid_length,
        hidden,
        w_key,
        w_value,
        w_query,
        key_cache,
        direct_wide,
        wide if direct_wide else 1,
    )
    keys = key_cache.reshape(slots, window * kv_local, head_dim)
    values = value_cache.reshape(slots, window * kv_local, head_dim)
    rows_out = w_out.shape[0]
    cut = rows_out // 4
    keys, values, w_first = fetch(
        [keys, values, w_out], ((0, 0, slots, 2), (1, 0, slots, 2), (2, 0, cut, 2)), bias
    )
    if direct_wide:
        parts = exchange(parts, "wide")
    else:
        parts = [lax.psum_scatter(parts[0], "wide", scatter_dimension=0, tiled=True)]
    heads, keys_out, values_out = attend(parts, keys, values, bias, kv_local, w_query.shape[1])
    (w_rest,) = fetch([w_out], ((0, cut, rows_out - cut, 6),), picks)
    if direct_wide:
        heads = exchange([heads] * wide, "wide")
    else:
        heads = [lax.all_gather(heads, "wide", axis=0, tiled=True)]
    narrow = lax.axis_size("narrow")
    direct_narrow = is_direct(narrow)
    sent = project_out(
        picks, heads, [w_first, w_rest], jnp.bfloat16 if direct_narrow else jnp.float32
    )
    if direct_narrow:
        attn_out = tree_sum([t.astype(jnp.float32) for t in exchange([sent] * narrow, "narrow")])
    else:
        attn_out = lax.psum(sent, "narrow")
    return (attn_out.astype(jnp.bfloat16), keys_out, values_out)


def solution(mesh):
    placed = (
        P("groups", "wide"),
        P("wide", "narrow"),
        P("wide", "narrow"),
        P("wide", "narrow"),
        P("narrow", "wide"),
        P(("groups", "wide"), None, "narrow", None),
        P(("groups", "wide"), None, "narrow", None),
        P(("groups", "wide")),
        P(("groups", "wide")),
        P("groups"),
    )
    return jax.shard_map(
        per_device,
        mesh=mesh,
        in_specs=placed,
        out_specs=(
            P("groups", "wide"),
            P(("groups", "wide"), "narrow"),
            P(("groups", "wide"), "narrow"),
        ),
        check_vma=False,
    )
```

```python
import functools

import jax
import jax.numpy as jnp
from jax import lax
from jax.experimental import pallas as pl
from jax.experimental.pallas import tpu as pltpu
from jax.sharding import PartitionSpec as P

masked_low = -1e30
most_direct = 8
depth_block = 512
mebibyte = 2**20

in_hbm = pl.BlockSpec(memory_space=pltpu.MemorySpace.HBM)
in_vmem = pl.BlockSpec(memory_space=pltpu.MemorySpace.VMEM)


def kept_in_hbm(x):
    return pltpu.with_memory_space_constraint(x, pltpu.MemorySpace.HBM)


def kept_in_vmem(x):
    return pltpu.with_memory_space_constraint(x, pltpu.MemorySpace.VMEM)


def is_direct(count):
    return count <= most_direct and count & (count - 1) == 0


def swap(block, axis, distance):
    count = lax.axis_size(axis)
    return lax.ppermute(block, axis, [(i, i ^ distance) for i in range(count)])


def exchange(blocks, axis):
    count = lax.axis_size(axis)
    came = [swap(blocks[d], axis, d) for d in range(count - 1, 0, -1)]
    return [blocks[0]] + came[::-1]


def tree_sum(terms):
    while len(terms) > 1:
        terms = [a + b for a, b in zip(terms[::2], terms[1::2])]
    return terms[0]


def project_kernel(slots_dev, direct, pieces, kv_local, *refs):
    ins, refs = refs[:8], refs[8:]
    slot_hbm, offset_hbm, length_hbm, hidden_hbm, wk_hbm, wv_hbm, wq_hbm, me_ref = ins
    outs, refs = refs[:pieces], refs[pieces:]
    picks_ref, bias_ref, slot, offset, length, hidden, wk, wv, wq, rows, total, small, large = refs
    depth = wq.shape[0]
    blocks = large.shape[0] - 2
    step = depth // blocks
    early = [
        pltpu.make_async_copy(source, target, small.at[i])
        for i, (source, target) in enumerate(
            ((slot_hbm, slot), (hidden_hbm, hidden), (offset_hbm, offset), (length_hbm, length))
        )
    ]
    query_cols, key_cols = wq.shape[1], wk.shape[1]
    plan = [
        (wk_hbm, wk, 0, depth, query_cols),
        (wv_hbm, wv, 0, depth, query_cols + key_cols),
    ] + [(wq_hbm, wq, b * step, step, 0) for b in range(blocks)]
    late = [
        pltpu.make_async_copy(
            source.at[pl.ds(first, size)], target.at[pl.ds(first, size)], large.at[i]
        )
        for i, (source, target, first, size, _) in enumerate(plan)
    ]
    for copy in early + late:
        copy.start()

    early[0].wait()
    early[1].wait()
    requests = slot.shape[1]
    place = lax.broadcasted_iota(jnp.int32, (requests, requests), 0)
    if direct:
        me = me_ref[0]
        slot_at = (me ^ (place // slots_dev)) * slots_dev + place % slots_dev
    else:
        slot_at = place
    picks = (slot_at == slot[...]).astype(jnp.float32).astype(jnp.bfloat16)
    picks_ref[...] = picks
    rows[...] = jnp.dot(picks, hidden[...], preferred_element_type=jnp.float32).astype(jnp.bfloat16)

    early[2].wait()
    early[3].wait()
    slots, places = bias_ref.shape
    window = places // kv_local
    position = lax.broadcasted_iota(jnp.int32, (1, places), 1) // kv_local
    for s in range(slots):
        gap = offset[s] - position
        distance = jnp.where(gap < 0, gap + window, gap)
        usable = (distance > 0) & (distance < length[s])
        bias_ref[s : s + 1, :] = jnp.where(usable, 0.0, masked_low)

    for copy, (_, weight, first, size, left) in zip(late, plan):
        copy.wait()
        span = pl.ds(first, size)
        right = left + weight.shape[1]
        part = jnp.dot(rows[:, span], weight[span, :], preferred_element_type=jnp.float32)
        if first == 0:
            total[:, left:right] = part
        else:
            total[:, left:right] += part
    size = requests // pieces
    for d, out in enumerate(outs[::-1]):
        out[...] = total[d * size : (d + 1) * size, :]


def project(me, slot_of, offset, length, hidden, w_key, w_value, w_query, cache, direct, pieces):
    requests = slot_of.shape[0]
    slots, places = cache.shape[0], cache.shape[1] * cache.shape[2]
    depth, query_cols = w_query.shape
    cols = query_cols + w_key.shape[1] + w_value.shape[1]
    blocks = max(1, depth // depth_block)
    found = pl.pallas_call(
        functools.partial(project_kernel, slots, direct, pieces, cache.shape[2]),
        out_shape=[pltpu.VMEM((requests // pieces, cols), jnp.float32) for _ in range(pieces)]
        + [pltpu.VMEM((requests, requests), jnp.bfloat16), pltpu.VMEM((slots, places), jnp.float32)],
        in_specs=[in_hbm] * 7 + [pl.BlockSpec(memory_space=pltpu.MemorySpace.SMEM)],
        out_specs=[in_vmem] * (pieces + 2),
        scratch_shapes=[
            pltpu.VMEM((1, requests), jnp.int32),
            pltpu.SMEM(offset.shape, jnp.int32),
            pltpu.SMEM(length.shape, jnp.int32),
            pltpu.VMEM(hidden.shape, jnp.bfloat16),
            pltpu.VMEM(w_key.shape, jnp.bfloat16),
            pltpu.VMEM(w_value.shape, jnp.bfloat16),
            pltpu.VMEM(w_query.shape, jnp.bfloat16),
            pltpu.VMEM(hidden.shape, jnp.bfloat16),
            pltpu.VMEM((requests, cols), jnp.float32),
            pltpu.SemaphoreType.DMA((4,)),
            pltpu.SemaphoreType.DMA((blocks + 2,)),
        ],
        compiler_params=pltpu.CompilerParams(vmem_limit_bytes=24 * mebibyte),
        cost_estimate=pl.CostEstimate(
            flops=2 * requests * depth * cols, bytes_accessed=2 * depth * cols, transcendentals=0
        ),
    )(
        *[
            kept_in_hbm(x)
            for x in (slot_of.reshape(1, -1), offset, length, hidden, w_key, w_value, w_query)
        ],
        me.reshape(1),
    )
    return found[:pieces][::-1], found[pieces], found[pieces + 1]


def attend_kernel(group, parts_count, kv_local, *refs):
    parts, refs = refs[:parts_count], refs[parts_count:]
    keys, values, bias, heads_ref, keys_ref, values_ref, query_rows, mixed_rows = refs
    slots, places, head_dim = keys.shape
    rows = kv_local * group
    query_cols, key_cols = rows * head_dim, kv_local * head_dim
    fresh = tree_sum([part[...] for part in parts]).astype(jnp.bfloat16)
    keys_ref[...] = fresh[:, query_cols : query_cols + key_cols]
    values_ref[...] = fresh[:, query_cols + key_cols :]
    fresh = fresh.astype(jnp.float32)
    for h in range(rows):
        query_rows[pl.ds(h, slots, stride=rows), :] = fresh[:, h * head_dim : (h + 1) * head_dim]
    scale = 1.0 / head_dim**0.5
    row_kv = lax.broadcasted_iota(jnp.int32, (rows, 1), 0) // group
    col_kv = lax.broadcasted_iota(jnp.int32, (1, places), 1) % kv_local
    own_head = row_kv == col_kv

    def spread_new(s, first):
        out = fresh[s : s + 1, first : first + head_dim]
        for k in range(1, kv_local):
            left = first + k * head_dim
            out = jnp.where(row_kv == k, fresh[s : s + 1, left : left + head_dim], out)
        return out

    every = range(slots)
    query = [query_rows[s * rows : (s + 1) * rows, :] for s in every]
    scores = [
        lax.dot_general(
            query[s].astype(jnp.bfloat16),
            keys[s],
            (((1,), (1,)), ((), ())),
            preferred_element_type=jnp.float32,
        )
        for s in every
    ]
    latest = [
        jnp.sum(query[s] * spread_new(s, query_cols), axis=1, keepdims=True) for s in every
    ]
    masked = [
        jnp.where(own_head & (bias[s : s + 1, :] == 0.0), scores[s], masked_low) for s in every
    ]
    top = [
        jnp.maximum(jnp.max(masked[s], axis=1, keepdims=True), latest[s]) for s in every
    ]
    spread = [jnp.exp((masked[s] - top[s]) * scale) for s in every]
    own = [jnp.exp((latest[s] - top[s]) * scale) for s in every]
    total = [jnp.sum(spread[s], axis=1, keepdims=True) + own[s] for s in every]
    mixed = [
        jnp.dot(spread[s].astype(jnp.bfloat16), values[s], preferred_element_type=jnp.float32)
        for s in every
    ]
    for s in every:
        mixed_rows[s * rows : (s + 1) * rows, :] = (
            mixed[s] + own[s] * spread_new(s, query_cols + key_cols)
        ) / total[s]
    for h in range(rows):
        heads_ref[:, h * head_dim : (h + 1) * head_dim] = mixed_rows[
            pl.ds(h, slots, stride=rows), :
        ].astype(jnp.bfloat16)


def attend(parts, keys, values, bias, kv_local, query_cols):
    slots, places, head_dim = keys.shape
    rows = query_cols // head_dim
    key_cols = kv_local * head_dim
    return pl.pallas_call(
        functools.partial(attend_kernel, rows // kv_local, len(parts), kv_local),
        out_shape=[
            pltpu.VMEM((slots, query_cols), jnp.bfloat16),
            pltpu.VMEM((slots, key_cols), jnp.bfloat16),
            pltpu.VMEM((slots, key_cols), jnp.bfloat16),
        ],
        in_specs=[in_vmem] * (len(parts) + 3),
        out_specs=[in_vmem] * 3,
        scratch_shapes=[
            pltpu.VMEM((slots * rows, head_dim), jnp.float32),
            pltpu.VMEM((slots * rows, head_dim), jnp.float32),
        ],
        compiler_params=pltpu.CompilerParams(vmem_limit_bytes=24 * mebibyte),
        cost_estimate=pl.CostEstimate(
            flops=4 * slots * rows * places * head_dim,
            bytes_accessed=4 * slots * places * head_dim,
            transcendentals=slots * rows * places,
        ),
    )(*[kept_in_vmem(x) for x in parts], keys, values, kept_in_vmem(bias))


def output_kernel(heads_count, picks_ref, keys_ref, values_ref, *refs):
    heads, weight, refs = refs[:heads_count], refs[heads_count], refs[heads_count + 1 :]
    out_ref, keys_hbm, values_hbm, sems = refs
    copies = [
        pltpu.make_async_copy(keys_ref, keys_hbm, sems.at[0]),
        pltpu.make_async_copy(values_ref, values_hbm, sems.at[1]),
    ]
    for copy in copies:
        copy.start()
    stacked = jnp.concatenate([h[...].astype(jnp.float32) for h in heads], axis=0)
    rows = lax.dot_general(
        picks_ref[...],
        stacked.astype(jnp.bfloat16),
        (((0,), (0,)), ((), ())),
        preferred_element_type=jnp.float32,
    ).astype(jnp.bfloat16)
    out_ref[...] = jnp.dot(rows, weight[...], preferred_element_type=jnp.float32).astype(
        out_ref.dtype
    )
    for copy in copies:
        copy.wait()


def project_out(picks, keys, values, heads, weight, dtype):
    requests = picks.shape[0]
    return pl.pallas_call(
        functools.partial(output_kernel, len(heads)),
        out_shape=[
            pltpu.VMEM((requests, weight.shape[1]), dtype),
            pltpu.MemorySpace.HBM(keys.shape, keys.dtype),
            pltpu.MemorySpace.HBM(values.shape, values.dtype),
        ],
        in_specs=[in_vmem] * (4 + len(heads)),
        out_specs=[in_vmem, in_hbm, in_hbm],
        scratch_shapes=[pltpu.SemaphoreType.DMA((2,))],
        compiler_params=pltpu.CompilerParams(vmem_limit_bytes=24 * mebibyte),
        cost_estimate=pl.CostEstimate(
            flops=2 * requests * weight.size, bytes_accessed=2 * weight.size, transcendentals=0
        ),
    )(*[kept_in_vmem(x) for x in (picks, keys, values, *heads)], weight)


def per_device(
    hidden,
    w_query,
    w_key,
    w_value,
    w_out,
    key_cache,
    value_cache,
    cycle_offset,
    valid_length,
    slot_of,
):
    slots, window, kv_local, head_dim = key_cache.shape
    wide = lax.axis_size("wide")
    direct_wide = is_direct(wide)
    me = lax.axis_index("wide").astype(jnp.int32)
    parts, picks, bias = project(
        me,
        slot_of,
        cycle_offset,
        valid_length,
        hidden,
        w_key,
        w_value,
        w_query,
        key_cache,
        direct_wide,
        wide if direct_wide else 1,
    )
    keys = key_cache.reshape(slots, window * kv_local, head_dim)
    values = value_cache.reshape(slots, window * kv_local, head_dim)
    if direct_wide:
        parts = exchange(parts, "wide")
    else:
        parts = [lax.psum_scatter(parts[0], "wide", scatter_dimension=0, tiled=True)]
    heads, keys_out, values_out = attend(parts[::-1], keys, values, bias, kv_local, w_query.shape[1])
    if direct_wide:
        heads = exchange([heads] * wide, "wide")
    else:
        heads = [lax.all_gather(heads, "wide", axis=0, tiled=True)]
    narrow = lax.axis_size("narrow")
    direct_narrow = is_direct(narrow)
    sent, keys_out, values_out = project_out(
        picks,
        keys_out,
        values_out,
        heads,
        w_out,
        jnp.bfloat16 if direct_narrow else jnp.float32,
    )
    if direct_narrow:
        distance = narrow // 2
        attn_out = sent
        while distance >= 1:
            attn_out = attn_out.astype(jnp.float32) + swap(attn_out, "narrow", distance).astype(jnp.float32)
            distance //= 2
            attn_out = attn_out.astype(jnp.bfloat16)
    else:
        attn_out = lax.psum(sent, "narrow")
    return (attn_out.astype(jnp.bfloat16), keys_out, values_out)


def solution(mesh):
    placed = (
        P("groups", "wide"),
        P("wide", "narrow"),
        P("wide", "narrow"),
        P("wide", "narrow"),
        P("narrow", "wide"),
        P(("groups", "wide"), None, "narrow", None),
        P(("groups", "wide"), None, "narrow", None),
        P(("groups", "wide")),
        P(("groups", "wide")),
        P("groups"),
    )
    return jax.shard_map(
        per_device,
        mesh=mesh,
        in_specs=placed,
        out_specs=(
            P("groups", "wide"),
            P(("groups", "wide"), "narrow"),
            P(("groups", "wide"), "narrow"),
        ),
        check_vma=False,
    )
```

```python
import functools

import jax
import jax.numpy as jnp
from jax import lax
from jax.experimental import pallas as pl
from jax.experimental.pallas import tpu as pltpu
from jax.sharding import PartitionSpec as P

masked_low = -1e30
most_direct = 8
depth_block = 512
mebibyte = 2**20

in_hbm = pl.BlockSpec(memory_space=pltpu.MemorySpace.HBM)
in_vmem = pl.BlockSpec(memory_space=pltpu.MemorySpace.VMEM)


def kept_in_hbm(x):
    return pltpu.with_memory_space_constraint(x, pltpu.MemorySpace.HBM)


def kept_in_vmem(x):
    return pltpu.with_memory_space_constraint(x, pltpu.MemorySpace.VMEM)


def is_direct(count):
    return count <= most_direct and count & (count - 1) == 0


def swap(block, axis, distance):
    count = lax.axis_size(axis)
    return lax.ppermute(block, axis, [(i, i ^ distance) for i in range(count)])


def exchange(blocks, axis):
    count = lax.axis_size(axis)
    came = [swap(blocks[d], axis, d) for d in range(count - 1, 0, -1)]
    return [blocks[0]] + came[::-1]


def cross(block, distance):
    wide, narrow = lax.axis_size("wide"), lax.axis_size("narrow")
    return lax.ppermute(
        block,
        ("wide", "narrow"),
        [
            (w * narrow + n, (w ^ distance) * narrow + (n ^ 1))
            for w in range(wide)
            for n in range(narrow)
        ],
    )


def cross_all(blocks):
    own = cross(blocks[0], 0)
    came = [cross(blocks[d], d) for d in range(len(blocks) - 1, 0, -1)]
    return [own] + came[::-1]


def tree_sum(terms):
    while len(terms) > 1:
        terms = [a + b for a, b in zip(terms[::2], terms[1::2])]
    return terms[0]


def project_kernel(slots_dev, direct, pieces, kv_local, *refs):
    ins, refs = refs[:8], refs[8:]
    slot_hbm, offset_hbm, length_hbm, hidden_hbm, wk_hbm, wv_hbm, wq_hbm, me_ref = ins
    outs, refs = refs[:pieces], refs[pieces:]
    picks_ref, bias_ref, slot, offset, length, hidden, wk, wv, wq, rows, total, small, large = refs
    depth = wq.shape[0]
    blocks = large.shape[0] - 2
    step = depth // blocks
    early = [
        pltpu.make_async_copy(source, target, small.at[i])
        for i, (source, target) in enumerate(
            ((slot_hbm, slot), (hidden_hbm, hidden), (offset_hbm, offset), (length_hbm, length))
        )
    ]
    query_cols, key_cols = wq.shape[1], wk.shape[1]
    plan = [
        (wk_hbm, wk, 0, depth, query_cols),
        (wv_hbm, wv, 0, depth, query_cols + key_cols),
    ] + [(wq_hbm, wq, b * step, step, 0) for b in range(blocks)]
    late = [
        pltpu.make_async_copy(
            source.at[pl.ds(first, size)], target.at[pl.ds(first, size)], large.at[i]
        )
        for i, (source, target, first, size, _) in enumerate(plan)
    ]
    for copy in early + late:
        copy.start()

    early[0].wait()
    early[1].wait()
    requests = slot.shape[1]
    place = lax.broadcasted_iota(jnp.int32, (requests, requests), 0)
    if direct:
        me = me_ref[0]
        slot_at = (me ^ (place // slots_dev)) * slots_dev + place % slots_dev
    else:
        slot_at = place
    picks = (slot_at == slot[...]).astype(jnp.float32).astype(jnp.bfloat16)
    picks_ref[...] = picks
    rows[...] = jnp.dot(picks, hidden[...], preferred_element_type=jnp.float32).astype(jnp.bfloat16)

    early[2].wait()
    early[3].wait()
    slots, places = bias_ref.shape
    window = places // kv_local
    position = lax.broadcasted_iota(jnp.int32, (1, places), 1) // kv_local
    for s in range(slots):
        gap = offset[s] - position
        distance = jnp.where(gap < 0, gap + window, gap)
        usable = (distance > 0) & (distance < length[s])
        bias_ref[s : s + 1, :] = jnp.where(usable, 0.0, masked_low)

    for copy, (_, weight, first, size, left) in zip(late, plan):
        copy.wait()
        span = pl.ds(first, size)
        right = left + weight.shape[1]
        part = jnp.dot(rows[:, span], weight[span, :], preferred_element_type=jnp.float32)
        if first == 0:
            total[:, left:right] = part
        else:
            total[:, left:right] += part
    size = requests // pieces
    for d, out in enumerate(outs[::-1]):
        out[...] = total[d * size : (d + 1) * size, :]


def project(me, slot_of, offset, length, hidden, w_key, w_value, w_query, cache, direct, pieces):
    requests = slot_of.shape[0]
    slots, places = cache.shape[0], cache.shape[1] * cache.shape[2]
    depth, query_cols = w_query.shape
    cols = query_cols + w_key.shape[1] + w_value.shape[1]
    blocks = max(1, depth // depth_block)
    found = pl.pallas_call(
        functools.partial(project_kernel, slots, direct, pieces, cache.shape[2]),
        out_shape=[pltpu.VMEM((requests // pieces, cols), jnp.float32) for _ in range(pieces)]
        + [pltpu.VMEM((requests, requests), jnp.bfloat16), pltpu.VMEM((slots, places), jnp.float32)],
        in_specs=[in_hbm] * 7 + [pl.BlockSpec(memory_space=pltpu.MemorySpace.SMEM)],
        out_specs=[in_vmem] * (pieces + 2),
        scratch_shapes=[
            pltpu.VMEM((1, requests), jnp.int32),
            pltpu.SMEM(offset.shape, jnp.int32),
            pltpu.SMEM(length.shape, jnp.int32),
            pltpu.VMEM(hidden.shape, jnp.bfloat16),
            pltpu.VMEM(w_key.shape, jnp.bfloat16),
            pltpu.VMEM(w_value.shape, jnp.bfloat16),
            pltpu.VMEM(w_query.shape, jnp.bfloat16),
            pltpu.VMEM(hidden.shape, jnp.bfloat16),
            pltpu.VMEM((requests, cols), jnp.float32),
            pltpu.SemaphoreType.DMA((4,)),
            pltpu.SemaphoreType.DMA((blocks + 2,)),
        ],
        compiler_params=pltpu.CompilerParams(vmem_limit_bytes=24 * mebibyte),
        cost_estimate=pl.CostEstimate(
            flops=2 * requests * depth * cols, bytes_accessed=2 * depth * cols, transcendentals=0
        ),
    )(
        *[
            kept_in_hbm(x)
            for x in (slot_of.reshape(1, -1), offset, length, hidden, w_key, w_value, w_query)
        ],
        me.reshape(1),
    )
    return found[:pieces][::-1], found[pieces], found[pieces + 1]


def attend_kernel(group, parts_count, kv_local, *refs):
    parts, refs = refs[:parts_count], refs[parts_count:]
    keys, values, bias, heads_ref, latest_ref, query_rows, mixed_rows = refs
    slots, places, head_dim = keys.shape
    rows = kv_local * group
    query_cols, key_cols = rows * head_dim, kv_local * head_dim
    fresh = tree_sum([part[...] for part in parts]).astype(jnp.bfloat16)
    latest_ref[...] = fresh[:, query_cols:]
    fresh = fresh.astype(jnp.float32)
    for h in range(rows):
        query_rows[pl.ds(h, slots, stride=rows), :] = fresh[:, h * head_dim : (h + 1) * head_dim]
    scale = 1.0 / head_dim**0.5
    row_kv = lax.broadcasted_iota(jnp.int32, (rows, 1), 0) // group
    col_kv = lax.broadcasted_iota(jnp.int32, (1, places), 1) % kv_local
    own_head = row_kv == col_kv

    def spread_new(s, first):
        out = fresh[s : s + 1, first : first + head_dim]
        for k in range(1, kv_local):
            left = first + k * head_dim
            out = jnp.where(row_kv == k, fresh[s : s + 1, left : left + head_dim], out)
        return out

    every = range(slots)
    query = [query_rows[s * rows : (s + 1) * rows, :] for s in every]
    scores = [
        lax.dot_general(
            query[s].astype(jnp.bfloat16),
            keys[s],
            (((1,), (1,)), ((), ())),
            preferred_element_type=jnp.float32,
        )
        for s in every
    ]
    latest = [
        jnp.sum(query[s] * spread_new(s, query_cols), axis=1, keepdims=True) for s in every
    ]
    masked = [
        jnp.where(own_head & (bias[s : s + 1, :] == 0.0), scores[s], masked_low) for s in every
    ]
    top = [
        jnp.maximum(jnp.max(masked[s], axis=1, keepdims=True), latest[s]) for s in every
    ]
    spread = [jnp.exp((masked[s] - top[s]) * scale) for s in every]
    own = [jnp.exp((latest[s] - top[s]) * scale) for s in every]
    total = [jnp.sum(spread[s], axis=1, keepdims=True) + own[s] for s in every]
    mixed = [
        jnp.dot(spread[s].astype(jnp.bfloat16), values[s], preferred_element_type=jnp.float32)
        for s in every
    ]
    for s in every:
        mixed_rows[s * rows : (s + 1) * rows, :] = (
            mixed[s] + own[s] * spread_new(s, query_cols + key_cols)
        ) / total[s]
    for h in range(rows):
        heads_ref[:, h * head_dim : (h + 1) * head_dim] = mixed_rows[
            pl.ds(h, slots, stride=rows), :
        ].astype(jnp.bfloat16)


def attend(parts, keys, values, bias, kv_local, query_cols):
    slots, places, head_dim = keys.shape
    rows = query_cols // head_dim
    key_cols = kv_local * head_dim
    return pl.pallas_call(
        functools.partial(attend_kernel, rows // kv_local, len(parts), kv_local),
        out_shape=[
            pltpu.VMEM((slots, query_cols), jnp.bfloat16),
            pltpu.VMEM((slots, 2 * key_cols), jnp.bfloat16),
        ],
        in_specs=[in_vmem] * (len(parts) + 3),
        out_specs=[in_vmem] * 2,
        scratch_shapes=[
            pltpu.VMEM((slots * rows, head_dim), jnp.float32),
            pltpu.VMEM((slots * rows, head_dim), jnp.float32),
        ],
        compiler_params=pltpu.CompilerParams(vmem_limit_bytes=24 * mebibyte),
        cost_estimate=pl.CostEstimate(
            flops=4 * slots * rows * places * head_dim,
            bytes_accessed=4 * slots * places * head_dim,
            transcendentals=slots * rows * places,
        ),
    )(*[kept_in_vmem(x) for x in parts], keys, values, kept_in_vmem(bias))


def output_kernel(heads_count, picks_ref, *refs):
    heads, (weight, out_ref) = refs[:heads_count], refs[heads_count:]
    stacked = jnp.concatenate([h[...].astype(jnp.float32) for h in heads], axis=0)
    rows = lax.dot_general(
        picks_ref[...],
        stacked.astype(jnp.bfloat16),
        (((0,), (0,)), ((), ())),
        preferred_element_type=jnp.float32,
    ).astype(jnp.bfloat16)
    out_ref[...] = jnp.dot(rows, weight[...], preferred_element_type=jnp.float32).astype(
        out_ref.dtype
    )


def project_out(picks, heads, weight, dtype):
    requests = picks.shape[0]
    return pl.pallas_call(
        functools.partial(output_kernel, len(heads)),
        out_shape=pltpu.VMEM((requests, weight.shape[1]), dtype),
        in_specs=[in_vmem] * (2 + len(heads)),
        out_specs=in_vmem,
        compiler_params=pltpu.CompilerParams(vmem_limit_bytes=24 * mebibyte),
        cost_estimate=pl.CostEstimate(
            flops=2 * requests * weight.size, bytes_accessed=2 * weight.size, transcendentals=0
        ),
    )(*[kept_in_vmem(x) for x in (picks, *heads)], weight)


def per_device(
    hidden,
    w_query,
    w_key,
    w_value,
    w_out,
    key_cache,
    value_cache,
    cycle_offset,
    valid_length,
    slot_of,
):
    slots, window, kv_local, head_dim = key_cache.shape
    wide = lax.axis_size("wide")
    direct_wide = is_direct(wide)
    me = lax.axis_index("wide").astype(jnp.int32)
    parts, picks, bias = project(
        me,
        slot_of,
        cycle_offset,
        valid_length,
        hidden,
        w_key,
        w_value,
        w_query,
        key_cache,
        direct_wide,
        wide if direct_wide else 1,
    )
    keys = key_cache.reshape(slots, window * kv_local, head_dim)
    values = value_cache.reshape(slots, window * kv_local, head_dim)
    if direct_wide:
        values, bias = lax.optimization_barrier((values, bias))
        keys, values = swap(keys, "narrow", 1), swap(values, "narrow", 1)
    if direct_wide:
        parts = cross_all(parts)
    else:
        parts = [lax.psum_scatter(parts[0], "wide", scatter_dimension=0, tiled=True)]
    heads, latest = attend(parts[::-1], keys, values, bias, kv_local, w_query.shape[1])
    if direct_wide:
        heads = cross_all([heads] * wide)
        latest = swap(latest, "narrow", 1)
    else:
        heads = [lax.all_gather(heads, "wide", axis=0, tiled=True)]
    narrow = lax.axis_size("narrow")
    direct_narrow = is_direct(narrow)
    sent = project_out(picks, heads, w_out, jnp.bfloat16 if direct_narrow else jnp.float32)
    if direct_narrow:
        attn_out = sent
        distance = narrow // 2
        while distance >= 1:
            came = swap(attn_out, "narrow", distance | 1)
            attn_out = (attn_out.astype(jnp.float32) + came.astype(jnp.float32)).astype(
                jnp.bfloat16
            )
            distance //= 2
    else:
        attn_out = lax.psum(sent, "narrow")
    key_cols = w_key.shape[1]
    return (attn_out.astype(jnp.bfloat16), latest[:, :key_cols], latest[:, key_cols:])


def solution(mesh):
    placed = (
        P("groups", "wide"),
        P("wide", "narrow"),
        P("wide", "narrow"),
        P("wide", "narrow"),
        P("narrow", "wide"),
        P(("groups", "wide"), None, "narrow", None),
        P(("groups", "wide"), None, "narrow", None),
        P(("groups", "wide")),
        P(("groups", "wide")),
        P("groups"),
    )
    return jax.shard_map(
        per_device,
        mesh=mesh,
        in_specs=placed,
        out_specs=(
            P("groups", "wide"),
            P(("groups", "wide"), "narrow"),
            P(("groups", "wide"), "narrow"),
        ),
        check_vma=False,
    )
```

```python
import functools

import jax
import jax.numpy as jnp
from jax import lax
from jax.experimental import pallas as pl
from jax.experimental.pallas import tpu as pltpu
from jax.sharding import PartitionSpec as P

masked_low = -1e30
most_direct = 8
depth_block = 512
mebibyte = 2**20

in_hbm = pl.BlockSpec(memory_space=pltpu.MemorySpace.HBM)
in_vmem = pl.BlockSpec(memory_space=pltpu.MemorySpace.VMEM)


def kept_in_hbm(x):
    return pltpu.with_memory_space_constraint(x, pltpu.MemorySpace.HBM)


def kept_in_vmem(x):
    return pltpu.with_memory_space_constraint(x, pltpu.MemorySpace.VMEM)


def is_direct(count):
    return count <= most_direct and count & (count - 1) == 0


def swap(block, axis, distance):
    count = lax.axis_size(axis)
    return lax.ppermute(block, axis, [(i, i ^ distance) for i in range(count)])


def exchange(blocks, axis):
    count = lax.axis_size(axis)
    came = [swap(blocks[d], axis, d) for d in range(count - 1, 0, -1)]
    return [blocks[0]] + came[::-1]


def tree_sum(terms):
    while len(terms) > 1:
        terms = [a + b for a, b in zip(terms[::2], terms[1::2])]
    return terms[0]


def project_kernel(slots_dev, direct, pieces, kv_local, *refs):
    ins, refs = refs[:8], refs[8:]
    slot_hbm, offset_hbm, length_hbm, hidden_hbm, wk_hbm, wv_hbm, wq_hbm, me_ref = ins
    outs, refs = refs[:pieces], refs[pieces:]
    picks_ref, bias_ref, slot, offset, length, hidden, wk, wv, wq, rows, total, small, large = refs
    depth = wq.shape[0]
    blocks = large.shape[0] - 2
    step = depth // blocks
    early = [
        pltpu.make_async_copy(source, target, small.at[i])
        for i, (source, target) in enumerate(
            ((slot_hbm, slot), (hidden_hbm, hidden), (offset_hbm, offset), (length_hbm, length))
        )
    ]
    query_cols, key_cols = wq.shape[1], wk.shape[1]
    plan = [
        (wk_hbm, wk, 0, depth, query_cols),
        (wv_hbm, wv, 0, depth, query_cols + key_cols),
    ] + [(wq_hbm, wq, b * step, step, 0) for b in range(blocks)]
    late = [
        pltpu.make_async_copy(
            source.at[pl.ds(first, size)], target.at[pl.ds(first, size)], large.at[i]
        )
        for i, (source, target, first, size, _) in enumerate(plan)
    ]
    for copy in early + late:
        copy.start()

    early[0].wait()
    early[1].wait()
    requests = slot.shape[1]
    place = lax.broadcasted_iota(jnp.int32, (requests, requests), 0)
    if direct:
        me = me_ref[0]
        slot_at = (me ^ (place // slots_dev)) * slots_dev + place % slots_dev
    else:
        slot_at = place
    picks = (slot_at == slot[...]).astype(jnp.float32).astype(jnp.bfloat16)
    picks_ref[...] = picks
    rows[...] = jnp.dot(picks, hidden[...], preferred_element_type=jnp.float32).astype(jnp.bfloat16)

    early[2].wait()
    early[3].wait()
    slots, places = bias_ref.shape
    window = places // kv_local
    position = lax.broadcasted_iota(jnp.int32, (1, places), 1) // kv_local
    for s in range(slots):
        gap = offset[s] - position
        distance = jnp.where(gap < 0, gap + window, gap)
        usable = (distance > 0) & (distance < length[s])
        bias_ref[s : s + 1, :] = jnp.where(usable, 0.0, masked_low)

    for copy, (_, weight, first, size, left) in zip(late, plan):
        copy.wait()
        span = pl.ds(first, size)
        right = left + weight.shape[1]
        part = jnp.dot(rows[:, span], weight[span, :], preferred_element_type=jnp.float32)
        if first == 0:
            total[:, left:right] = part
        else:
            total[:, left:right] += part
    size = requests // pieces
    for d, out in enumerate(outs[::-1]):
        out[...] = total[d * size : (d + 1) * size, :]


def project(me, slot_of, offset, length, hidden, w_key, w_value, w_query, cache, direct, pieces):
    requests = slot_of.shape[0]
    slots, places = cache.shape[0], cache.shape[1] * cache.shape[2]
    depth, query_cols = w_query.shape
    cols = query_cols + w_key.shape[1] + w_value.shape[1]
    blocks = max(1, depth // depth_block)
    found = pl.pallas_call(
        functools.partial(project_kernel, slots, direct, pieces, cache.shape[2]),
        out_shape=[pltpu.VMEM((requests // pieces, cols), jnp.float32) for _ in range(pieces)]
        + [pltpu.VMEM((requests, requests), jnp.bfloat16), pltpu.VMEM((slots, places), jnp.float32)],
        in_specs=[in_hbm] * 7 + [pl.BlockSpec(memory_space=pltpu.MemorySpace.SMEM)],
        out_specs=[in_vmem] * (pieces + 2),
        scratch_shapes=[
            pltpu.VMEM((1, requests), jnp.int32),
            pltpu.SMEM(offset.shape, jnp.int32),
            pltpu.SMEM(length.shape, jnp.int32),
            pltpu.VMEM(hidden.shape, jnp.bfloat16),
            pltpu.VMEM(w_key.shape, jnp.bfloat16),
            pltpu.VMEM(w_value.shape, jnp.bfloat16),
            pltpu.VMEM(w_query.shape, jnp.bfloat16),
            pltpu.VMEM(hidden.shape, jnp.bfloat16),
            pltpu.VMEM((requests, cols), jnp.float32),
            pltpu.SemaphoreType.DMA((4,)),
            pltpu.SemaphoreType.DMA((blocks + 2,)),
        ],
        compiler_params=pltpu.CompilerParams(vmem_limit_bytes=24 * mebibyte),
        cost_estimate=pl.CostEstimate(
            flops=2 * requests * depth * cols, bytes_accessed=2 * depth * cols, transcendentals=0
        ),
    )(
        *[
            kept_in_hbm(x)
            for x in (slot_of.reshape(1, -1), offset, length, hidden, w_key, w_value, w_query)
        ],
        me.reshape(1),
    )
    return found[:pieces][::-1], found[pieces], found[pieces + 1]


def attend_kernel(group, parts_count, kv_local, *refs):
    parts, refs = refs[:parts_count], refs[parts_count:]
    keys, values, bias, heads_ref, keys_ref, values_ref, query_rows, mixed_rows = refs
    slots, places, head_dim = keys.shape
    rows = kv_local * group
    query_cols, key_cols = rows * head_dim, kv_local * head_dim
    fresh = tree_sum([part[...] for part in parts]).astype(jnp.bfloat16)
    keys_ref[...] = fresh[:, query_cols : query_cols + key_cols]
    values_ref[...] = fresh[:, query_cols + key_cols :]
    fresh = fresh.astype(jnp.float32)
    for h in range(rows):
        query_rows[pl.ds(h, slots, stride=rows), :] = fresh[:, h * head_dim : (h + 1) * head_dim]
    scale = 1.0 / head_dim**0.5
    row_kv = lax.broadcasted_iota(jnp.int32, (rows, 1), 0) // group
    col_kv = lax.broadcasted_iota(jnp.int32, (1, places), 1) % kv_local
    own_head = row_kv == col_kv

    def spread_new(s, first):
        out = fresh[s : s + 1, first : first + head_dim]
        for k in range(1, kv_local):
            left = first + k * head_dim
            out = jnp.where(row_kv == k, fresh[s : s + 1, left : left + head_dim], out)
        return out

    every = range(slots)
    query = [query_rows[s * rows : (s + 1) * rows, :] for s in every]
    scores = [
        lax.dot_general(
            query[s].astype(jnp.bfloat16),
            keys[s],
            (((1,), (1,)), ((), ())),
            preferred_element_type=jnp.float32,
        )
        for s in every
    ]
    latest = [
        jnp.sum(query[s] * spread_new(s, query_cols), axis=1, keepdims=True) for s in every
    ]
    masked = [
        jnp.where(own_head & (bias[s : s + 1, :] == 0.0), scores[s], masked_low) for s in every
    ]
    top = [
        jnp.maximum(jnp.max(masked[s], axis=1, keepdims=True), latest[s]) for s in every
    ]
    spread = [jnp.exp((masked[s] - top[s]) * scale) for s in every]
    own = [jnp.exp((latest[s] - top[s]) * scale) for s in every]
    total = [jnp.sum(spread[s], axis=1, keepdims=True) + own[s] for s in every]
    mixed = [
        jnp.dot(
            (spread[s] / total[s]).astype(jnp.bfloat16),
            values[s],
            preferred_element_type=jnp.float32,
        )
        for s in every
    ]
    for s in every:
        mixed_rows[s * rows : (s + 1) * rows, :] = (
            mixed[s] + own[s] / total[s] * spread_new(s, query_cols + key_cols)
        )
    for h in range(rows):
        heads_ref[:, h * head_dim : (h + 1) * head_dim] = mixed_rows[
            pl.ds(h, slots, stride=rows), :
        ].astype(jnp.bfloat16)


def attend(parts, keys, values, bias, kv_local, query_cols):
    slots, places, head_dim = keys.shape
    rows = query_cols // head_dim
    key_cols = kv_local * head_dim
    return pl.pallas_call(
        functools.partial(attend_kernel, rows // kv_local, len(parts), kv_local),
        out_shape=[
            pltpu.VMEM((slots, query_cols), jnp.bfloat16),
            pltpu.VMEM((slots, key_cols), jnp.bfloat16),
            pltpu.VMEM((slots, key_cols), jnp.bfloat16),
        ],
        in_specs=[in_vmem] * (len(parts) + 3),
        out_specs=[in_vmem] * 3,
        scratch_shapes=[
            pltpu.VMEM((slots * rows, head_dim), jnp.float32),
            pltpu.VMEM((slots * rows, head_dim), jnp.float32),
        ],
        compiler_params=pltpu.CompilerParams(vmem_limit_bytes=24 * mebibyte),
        cost_estimate=pl.CostEstimate(
            flops=4 * slots * rows * places * head_dim,
            bytes_accessed=4 * slots * places * head_dim,
            transcendentals=slots * rows * places,
        ),
    )(*[kept_in_vmem(x) for x in parts], keys, values, kept_in_vmem(bias))


def output_kernel(heads_count, picks_ref, keys_ref, values_ref, *refs):
    heads, weight, refs = refs[:heads_count], refs[heads_count], refs[heads_count + 1 :]
    out_ref, keys_hbm, values_hbm, sems = refs
    copies = [
        pltpu.make_async_copy(keys_ref, keys_hbm, sems.at[0]),
        pltpu.make_async_copy(values_ref, values_hbm, sems.at[1]),
    ]
    for copy in copies:
        copy.start()
    stacked = jnp.concatenate([h[...].astype(jnp.float32) for h in heads], axis=0)
    rows = lax.dot_general(
        picks_ref[...],
        stacked.astype(jnp.bfloat16),
        (((0,), (0,)), ((), ())),
        preferred_element_type=jnp.float32,
    ).astype(jnp.bfloat16)
    out_ref[...] = jnp.dot(rows, weight[...], preferred_element_type=jnp.float32).astype(
        out_ref.dtype
    )
    for copy in copies:
        copy.wait()


def project_out(picks, keys, values, heads, weight, dtype):
    requests = picks.shape[0]
    return pl.pallas_call(
        functools.partial(output_kernel, len(heads)),
        out_shape=[
            pltpu.VMEM((requests, weight.shape[1]), dtype),
            pltpu.MemorySpace.HBM(keys.shape, keys.dtype),
            pltpu.MemorySpace.HBM(values.shape, values.dtype),
        ],
        in_specs=[in_vmem] * (4 + len(heads)),
        out_specs=[in_vmem, in_hbm, in_hbm],
        scratch_shapes=[pltpu.SemaphoreType.DMA((2,))],
        compiler_params=pltpu.CompilerParams(vmem_limit_bytes=24 * mebibyte),
        cost_estimate=pl.CostEstimate(
            flops=2 * requests * weight.size, bytes_accessed=2 * weight.size, transcendentals=0
        ),
    )(*[kept_in_vmem(x) for x in (picks, keys, values, *heads)], weight)


def per_device(
    hidden,
    w_query,
    w_key,
    w_value,
    w_out,
    key_cache,
    value_cache,
    cycle_offset,
    valid_length,
    slot_of,
):
    slots, window, kv_local, head_dim = key_cache.shape
    wide = lax.axis_size("wide")
    direct_wide = is_direct(wide)
    me = lax.axis_index("wide").astype(jnp.int32)
    parts, picks, bias = project(
        me,
        slot_of,
        cycle_offset,
        valid_length,
        hidden,
        w_key,
        w_value,
        w_query,
        key_cache,
        direct_wide,
        wide if direct_wide else 1,
    )
    keys = key_cache.reshape(slots, window * kv_local, head_dim)
    values = value_cache.reshape(slots, window * kv_local, head_dim)
    if direct_wide:
        parts = exchange(parts, "wide")
    else:
        parts = [lax.psum_scatter(parts[0], "wide", scatter_dimension=0, tiled=True)]
    heads, keys_out, values_out = attend(parts[::-1], keys, values, bias, kv_local, w_query.shape[1])
    if direct_wide:
        heads = exchange([heads] * wide, "wide")
    else:
        heads = [lax.all_gather(heads, "wide", axis=0, tiled=True)]
    narrow = lax.axis_size("narrow")
    direct_narrow = is_direct(narrow)
    sent, keys_out, values_out = project_out(
        picks,
        keys_out,
        values_out,
        heads,
        w_out,
        jnp.bfloat16 if direct_narrow else jnp.float32,
    )
    if direct_narrow:
        distance = narrow // 2
        attn_out = sent
        while distance >= 1:
            attn_out = attn_out.astype(jnp.float32) + swap(attn_out, "narrow", distance).astype(jnp.float32)
            distance //= 2
            attn_out = attn_out.astype(jnp.bfloat16)
    else:
        attn_out = lax.psum(sent, "narrow")
    return (attn_out.astype(jnp.bfloat16), keys_out, values_out)


def solution(mesh):
    placed = (
        P("groups", "wide"),
        P("wide", "narrow"),
        P("wide", "narrow"),
        P("wide", "narrow"),
        P("narrow", "wide"),
        P(("groups", "wide"), None, "narrow", None),
        P(("groups", "wide"), None, "narrow", None),
        P(("groups", "wide")),
        P(("groups", "wide")),
        P("groups"),
    )
    return jax.shard_map(
        per_device,
        mesh=mesh,
        in_specs=placed,
        out_specs=(
            P("groups", "wide"),
            P(("groups", "wide"), "narrow"),
            P(("groups", "wide"), "narrow"),
        ),
        check_vma=False,
    )
```
